32 devices in a mesh: row: 4 (over y, x), col: 8 (over z, core).
Axes of the slice: x: 2, y: 2, z: 4, core: 2. Of those that a mesh axis runs over, the one named last changes fastest.
Arguments:
- spectra: bfloat16 [1024, 8, 1536], P(('row', 'col')), may hold values from -6 to 6
- pair_bins: int32 [4, 1024, 32], P(None, ('row', 'col')), may hold values from 0 to 127
- dead_mask: int32 [1024], P(('row', 'col')), may hold values 0 or 1
Outputs:
- stacked_lags: float32 [128, 896], P(('row', 'col'))
The draws below stay inside these ranges and needn't reach their ends.
All inputs are finite; a program needn't handle non-finite values. No bound on the sum of `dead_mask` on one device may be relied on, other than what follows from the above.
Results may differ from the reference program's by a relative error of at most 0.0041.
Values may be sent and summed in bfloat16 or wider, within the bound.
No kernel may reach another device: no remote copies, remote signals or barrier semaphores. Data moves between devices by JAX's collectives and lax.ppermute only.
A program may use at most 256 MiB of HBM per device.

```python
import math
import jax
import jax.numpy as jnp
from jax import lax

CB = 32
W = 8
F = 768
NT = 1600
LAGS = 896
NB = 128
ROUNDS = 4
CHANNELS = 1024
N_ROW = 4
N_COL = 8


def with_ends(entries, rng, smallest, high):
    extent = entries.shape
    index_at = [jax.random.randint(jax.random.fold_in(rng, axis), (), 0, extent[axis]) for axis in range(len(extent))]
    entries = entries.at[tuple(index_at)].set(smallest)
    longest = extent.index(max(extent))
    index_at[longest] = (index_at[longest] + 1) % extent[longest]
    return entries.at[tuple(index_at)].set(high)


def steps_of(rng, extent, split, low, largest):
    def one(axis_at, parts):
        draws = jax.random.uniform(jax.random.fold_in(jax.random.fold_in(rng, 6), axis_at), (parts,), jnp.float32, low / len(split), largest / len(split))
        return jnp.repeat(jnp.exp(draws), extent[axis_at] // parts).reshape((-1,) + (1,) * (len(extent) - axis_at - 1))

    loudness = one(*split[0])
    for cut in split[1:]:
        loudness = loudness * one(*cut)
    return loudness


def noise(rng, shape, deviation, limit, pieces=(), held_as=jnp.bfloat16):
    level = steps_of(rng, shape, pieces, -0.22, 0.18) if pieces else 1.0
    array = jax.random.normal(rng, shape, jnp.float32) * deviation * level
    return jnp.minimum(jnp.maximum(array, -limit), limit).astype(held_as)


def setup_inputs(seed: int = 0) -> dict:
    splits = jax.random.split(jax.random.key(seed), 4)
    return {
        "spectra": noise(splits[0], (CHANNELS, W, 2 * F), 1.0, 6.0, ((0, 32),)),
        "pair_bins": with_ends(jax.random.randint(splits[1], (ROUNDS, CHANNELS, CB), 0, NB), jax.random.fold_in(splits[1], 1), 0, NB - 1).astype(jnp.int32),
        "dead_mask": with_ends((jax.random.randint(splits[2], (CHANNELS,), 0, 8) < 7).astype(jnp.int32), jax.random.fold_in(splits[2], 1), 0, 1),
    }


def whiten(spectra, dead_mask):
    values = spectra.astype(jnp.float32)
    powers = lax.optimization_barrier(jnp.mean(values * values, axis=-1, keepdims=True))
    alive = dead_mask.astype(jnp.float32)[:, None, None]
    return (values / jnp.sqrt(powers + 1e-06) * alive).astype(jnp.bfloat16)

def cross_spectra(local_part, remote_part):
    half_len = local_part.shape[-1] // 2
    first = local_part.astype(jnp.float32)
    second = remote_part.astype(jnp.float32)
    high = lax.Precision.HIGHEST
    one_real, one_imag = (first[..., :half_len], first[..., half_len:])
    two_real, two_imag = (second[..., :half_len], second[..., half_len:])
    real_part = jnp.einsum('iwk,jwk->ijk', one_real, two_real, precision=high) + jnp.einsum('iwk,jwk->ijk', one_imag, two_imag, precision=high)
    imag_part = jnp.einsum('iwk,jwk->ijk', one_imag, two_real, precision=high) - jnp.einsum('iwk,jwk->ijk', one_real, two_imag, precision=high)
    channels = local_part.shape[0]
    return jnp.concatenate([real_part, imag_part], axis=-1).reshape(channels * remote_part.shape[0], 2 * half_len)

def build_table(freq_len, lag_len, length):
    freq_ids = jnp.arange(freq_len, dtype=jnp.int32)
    lag_ids = jnp.arange(lag_len, dtype=jnp.int32) - lag_len // 2
    phases = freq_ids[:, None] * lag_ids[None, :] % length
    angles = phases.astype(jnp.float32) * (2.0 * math.pi / length)
    weights = jnp.where(freq_ids == 0, 1.0, 2.0).astype(jnp.float32)[:, None]
    return jnp.concatenate([weights * jnp.cos(angles), -weights * jnp.sin(angles)], axis=0)

def reference(spectra, pair_bins, dead_mask):
    whitened = whiten(spectra, dead_mask)
    groups = N_ROW * N_COL
    block_size = spectra.shape[0] // groups
    freq_len = spectra.shape[2] // 2
    width = spectra.shape[1]

    def step_fn(stacked, position):
        round_no = position // groups
        device = position % groups
        partner = jnp.bitwise_xor(device, jnp.left_shift(jnp.int32(1), round_no)).astype(jnp.int32)
        local_part = lax.dynamic_slice_in_dim(whitened, (device * block_size).astype(jnp.int32), block_size, 0)
        remote_part = lax.dynamic_slice_in_dim(whitened, (partner * block_size).astype(jnp.int32), block_size, 0)
        bin_ids = lax.dynamic_slice(pair_bins, (round_no.astype(jnp.int32), (device * block_size).astype(jnp.int32), jnp.int32(0)), (1, block_size, block_size)).reshape(-1)
        stacked = stacked + jax.ops.segment_sum(cross_spectra(local_part, remote_part), bin_ids, num_segments=NB)
        return (stacked, None)
    start = jnp.zeros((NB, 2 * freq_len), jnp.float32)
    stacked, _ = lax.scan(step_fn, start, jnp.arange(ROUNDS * groups, dtype=jnp.int32))
    pairs = ROUNDS * block_size * block_size * groups // NB
    scaling = 1.0 / (2.0 * math.sqrt(freq_len * width * pairs))
    table = build_table(freq_len, LAGS, NT)
    return jnp.dot(stacked, table, precision=lax.Precision.HIGHEST) * scaling
```

```python
import functools
import math

import jax
import jax.numpy as jnp
import numpy as np
from jax import lax
from jax.experimental import pallas as pl
from jax.experimental.pallas import tpu as pltpu
from jax.sharding import PartitionSpec as P

NT = 1600
LAGS = 896
NB = 128
ROUNDS = 4
LANES = 128
AXES = ("row", "col")
F32 = jnp.float32
BF16 = jnp.bfloat16
VMEM_LIMIT = 48 * 2**20


def parity_of(index):
    total = 0
    for bit in range(ROUNDS):
        total = total + ((index >> bit) & 1)
    return total % 2


def swapped(value, stride, groups):
    mask = 2**stride
    return lax.ppermute(value, AXES, [(source, source ^ mask) for source in range(groups)])


def one_hot(rows, columns, row_offset, of_column):
    row_ids = lax.broadcasted_iota(jnp.int32, (rows, columns), 0)
    column_ids = lax.broadcasted_iota(jnp.int32, (rows, columns), 1)
    return (row_ids == row_offset + of_column(column_ids)).astype(BF16)


def pack_kernel(half_ref, spectra_ref, bins_ref, alive_ref, send_ref, keep_ref, scaled_ref):
    block, width, columns = spectra_ref.shape
    freq_len = columns // 2
    tiles = freq_len // 2 // LANES
    values = spectra_ref[...].astype(F32)
    powers = jnp.mean(values * values, axis=-1, keepdims=True)
    scaled_ref[...] = values * (lax.rsqrt(powers + 1e-06) * alive_ref[...])
    half = half_ref[0]
    for tile in range(tiles):
        for window in range(width):
            for part in range(2):
                plane = (tile * width + window) * 2 + part
                base = part * freq_len + tile * LANES
                mine = pl.multiple_of(base + half * (freq_len // 2), LANES)
                other = pl.multiple_of(base + (1 - half) * (freq_len // 2), LANES)
                kept = scaled_ref[:, window, pl.ds(mine, LANES)]
                keep_ref[plane] = kept.astype(BF16).astype(F32)
                send_ref[plane] = scaled_ref[:, window, pl.ds(other, LANES)].astype(BF16)
    rounds = bins_ref.shape[0]
    plane = jnp.zeros((block, LANES), F32)
    for round_no in range(rounds):
        place = one_hot(block, LANES, -block * round_no, lambda ids: ids)
        plane = plane + jnp.dot(bins_ref[round_no].astype(F32).astype(BF16), place, preferred_element_type=F32)
    send_ref[send_ref.shape[0] - 1] = plane.astype(BF16)


def pack(half, spectra, bins, alive):
    block, width, columns = spectra.shape
    planes = columns // 2 // LANES * width
    return pl.pallas_call(
        pack_kernel,
        out_shape=(
            jax.ShapeDtypeStruct((planes + 1, block, LANES), BF16),
            jax.ShapeDtypeStruct((planes, block, LANES), F32),
        ),
        in_specs=[pl.BlockSpec(memory_space=pltpu.SMEM)] + [pl.BlockSpec(memory_space=pltpu.VMEM)] * 3,
        out_specs=(pl.BlockSpec(memory_space=pltpu.VMEM),) * 2,
        scratch_shapes=[pltpu.VMEM((block, width, columns), F32)],
        compiler_params=pltpu.CompilerParams(vmem_limit_bytes=VMEM_LIMIT),
        name="pack",
    )(half, spectra, bins, alive)


def hot_pairs(mine, theirs, round_no, block):
    pairs = block * block
    base = block * round_no
    rows = lax.broadcasted_iota(jnp.int32, (block, pairs), 0)
    columns = lax.broadcasted_iota(jnp.int32, (block, pairs), 1)
    by_second = jnp.dot(mine, one_hot(LANES, pairs, base, lambda ids: ids % block), preferred_element_type=F32)
    by_first = jnp.dot(theirs, one_hot(LANES, pairs, base, lambda ids: ids // block), preferred_element_type=F32)
    first = jnp.sum(jnp.where(rows == columns // block, by_second, 0.0), axis=0, keepdims=True)
    second = jnp.sum(jnp.where(rows == columns % block, by_first, 0.0), axis=0, keepdims=True)
    bin_ids = lax.broadcasted_iota(jnp.int32, (NB, pairs), 0).astype(F32)
    hot_first = (bin_ids == first).astype(F32)
    hot_second = (bin_ids == second).astype(F32)
    return (hot_first + hot_second).astype(BF16), (hot_first - hot_second).astype(BF16)


def round_kernel(round_no, groups, keep_ref, send_ref, got_ref, total_ref, out_ref, plus_ref, minus_ref, real_ref, imag_ref):
    planes, block, _ = keep_ref.shape
    width = real_ref.shape[0] * groups
    tiles = planes // (2 * width)
    rows = 16
    plus, minus = hot_pairs(send_ref[planes], got_ref[planes], round_no, block)
    plus_ref[...] = plus
    minus_ref[...] = minus

    def of_channel(channel, carry):
        for tile in range(tiles):
            ones = [
                jnp.broadcast_to(keep_ref[tile * 2 * width + k, pl.ds(channel, 1), :], (rows, LANES)).astype(BF16)
                for k in range(2 * width)
            ]
            lanes = slice(tile * LANES, (tile + 1) * LANES)
            for start in range(0, block, rows):
                twos = [got_ref[tile * 2 * width + k, start : start + rows, :] for k in range(2 * width)]
                at = pl.ds(pl.multiple_of(channel * block + start, rows), rows)
                for part in range(width // groups):
                    real, imag = None, None
                    for window in range(part * groups, (part + 1) * groups):
                        one_real, one_imag = ones[2 * window], ones[2 * window + 1]
                        two_real, two_imag = twos[2 * window], twos[2 * window + 1]
                        more_real = one_real * two_real + one_imag * two_imag
                        more_imag = one_imag * two_real - one_real * two_imag
                        real = more_real if real is None else real + more_real
                        imag = more_imag if imag is None else imag + more_imag
                    real_ref[part, at, lanes] = real
                    imag_ref[part, at, lanes] = imag
        return carry

    lax.fori_loop(0, block, of_channel, 0)
    half = tiles * LANES
    real = total_ref[:, :half].astype(F32)
    imag = total_ref[:, half:].astype(F32)
    for part in range(width // groups):
        real = real + jnp.dot(plus_ref[...], real_ref[part], preferred_element_type=F32)
        imag = imag + jnp.dot(minus_ref[...], imag_ref[part], preferred_element_type=F32)
    out_ref[:, :half] = real.astype(out_ref.dtype)
    out_ref[:, half:] = imag.astype(out_ref.dtype)


def add_round(round_no, width, keep, send, got, total, out_dtype, groups=2):
    planes, block, _ = keep.shape
    half = planes // (2 * width) * LANES
    pairs = block * block
    return pl.pallas_call(
        functools.partial(round_kernel, round_no, groups),
        out_shape=jax.ShapeDtypeStruct((NB, 2 * half), out_dtype),
        in_specs=[pl.BlockSpec(memory_space=pltpu.VMEM)] * 4,
        out_specs=pl.BlockSpec(memory_space=pltpu.VMEM),
        scratch_shapes=[
            pltpu.VMEM((NB, pairs), BF16),
            pltpu.VMEM((NB, pairs), BF16),
            pltpu.VMEM((width // groups, pairs, half), BF16),
            pltpu.VMEM((width // groups, pairs, half), BF16),
        ],
        compiler_params=pltpu.CompilerParams(vmem_limit_bytes=VMEM_LIMIT),
        cost_estimate=pl.CostEstimate(flops=2 * 10**9, bytes_accessed=3 * 10**6, transcendentals=0),
        name="add_round",
    )(keep, send, got, total)


def lag_kernel(scaling, parities, parts_ref, high_ref, low_ref, out_ref):
    sums = []
    for half in range(2):
        total = None
        for source, parity in enumerate(parities):
            if parity == half:
                part = parts_ref[source].astype(F32)
                total = part if total is None else total + part
        sums.append(total)
    values = jnp.concatenate(sums, axis=1)
    high = values.astype(BF16)
    low = (values - high.astype(F32)).astype(BF16)
    table = high_ref[...]
    result = jnp.dot(high, table, preferred_element_type=F32)
    result = result + jnp.dot(low, table, preferred_element_type=F32)
    result = result + jnp.dot(high, low_ref[...], preferred_element_type=F32)
    out_ref[...] = result * scaling


def to_lags(parts, parities, scaling, high, low):
    return pl.pallas_call(
        functools.partial(lag_kernel, scaling, parities),
        out_shape=jax.ShapeDtypeStruct((parts.shape[1], LAGS), F32),
        in_specs=[pl.BlockSpec(memory_space=pltpu.VMEM)] * 3,
        out_specs=pl.BlockSpec(memory_space=pltpu.VMEM),
        compiler_params=pltpu.CompilerParams(vmem_limit_bytes=VMEM_LIMIT),
        name="to_lags",
    )(parts, high, low)


def build_table(freq_len):
    freq_ids = np.arange(freq_len).reshape(2, 1, freq_len // 2)
    lag_ids = np.arange(LAGS) - LAGS // 2
    angles = (freq_ids[..., None] * lag_ids % NT) * (2.0 * math.pi / NT)
    weights = np.where(freq_ids == 0, 1.0, 2.0)[..., None]
    table = np.concatenate([weights * np.cos(angles), -weights * np.sin(angles)], axis=1)
    table = table.reshape(2 * freq_len, LAGS).astype(np.float32)
    high = table.astype(BF16)
    return high, (table - high.astype(np.float32)).astype(BF16)


def on_device(spectra, pair_bins, dead_mask):
    block, width, columns = spectra.shape
    freq_len = columns // 2
    groups = lax.axis_size("row") * lax.axis_size("col")
    half = parity_of(lax.axis_index(AXES)).astype(jnp.int32)[None]
    alive = dead_mask.astype(F32)[:, None, None]
    send, keep = pack(half, spectra, pair_bins, alive)
    got = [swapped(send, round_no, groups) for round_no in range(ROUNDS)]
    total = jnp.zeros((NB, freq_len), F32)
    order = (0, 3, 1, 2)
    for round_no in order:
        last = round_no == order[-1]
        total = add_round(round_no, width, keep, send, got[round_no], total, BF16 if last else F32)
    mine = lax.all_to_all(total.reshape(groups, NB // groups, freq_len), AXES, 0, 0, tiled=True)
    pairs = ROUNDS * block * block * groups // NB
    scaling = 1.0 / (2.0 * math.sqrt(freq_len * width * pairs))
    high, low = build_table(freq_len)
    parities = [parity_of(source) for source in range(groups)]
    return to_lags(mine, parities, scaling, jnp.asarray(high), jnp.asarray(low))


def solution(mesh):
    return jax.shard_map(
        on_device,
        mesh=mesh,
        in_specs=(P(AXES, None, None), P(None, AXES, None), P(AXES)),
        out_specs=P(AXES, None),
        check_vma=False,
    )
```

```python
import functools
import math

import jax
import jax.numpy as jnp
import numpy as np
from jax import lax
from jax.experimental import pallas as pl
from jax.experimental.pallas import tpu as pltpu
from jax.sharding import PartitionSpec as P

NT = 1600
LAGS = 896
NB = 128
ROUNDS = 4
LANES = 128
ROWS = 16
SUMMED = 2
AXES = ("row", "col")
F32 = jnp.float32
BF16 = jnp.bfloat16
VMEM = pl.BlockSpec(memory_space=pltpu.VMEM)
HBM = pl.BlockSpec(memory_space=pltpu.MemorySpace.HBM)
LARGE = pltpu.CompilerParams(vmem_limit_bytes=63488 * 2**10)
PARAMS = pltpu.CompilerParams(vmem_limit_bytes=48 * 2**20)


def parity_of(index):
    total = 0
    for bit in range(ROUNDS):
        total = total + ((index >> bit) & 1)
    return total % 2


def half_here():
    return parity_of(lax.axis_index("row") * lax.axis_size("col") + lax.axis_index("col"))


def swapped(value, stride, groups):
    mask = 2**stride
    return lax.ppermute(value, AXES, [(source, source ^ mask) for source in range(groups)])


def one_hot(rows, columns, row_offset, of_column):
    row_ids = lax.broadcasted_iota(jnp.int32, (rows, columns), 0)
    column_ids = lax.broadcasted_iota(jnp.int32, (rows, columns), 1)
    return (row_ids == row_offset + of_column(column_ids)).astype(BF16)


def plane_of(scaled_ref, plane, block, half):
    tiles, width = scaled_ref.shape[0] // 4, scaled_ref.shape[1] // block
    tile, window, part = plane // (2 * width), plane // 2 % width, plane % 2
    return scaled_ref[2 * tiles * part + tiles * half + tile, pl.ds(window, block, stride=width), :]


def whiten_kernel(spectra_ref, bins_ref, alive_ref, *refs):
    first_ref, second_ref, whole_ref, keep_ref, scaled_ref, loaded_ref, loaded_bins_ref, loaded_alive_ref, sems = refs
    block, width, columns = spectra_ref.shape
    step = 8
    copies = [
        pltpu.make_async_copy(spectra_ref.at[pl.ds(at, step)], loaded_ref.at[pl.ds(at, step)], sems.at[at // step])
        for at in range(0, block, step)
    ]
    bins_copy = pltpu.make_async_copy(bins_ref, loaded_bins_ref, sems.at[block // step])
    alive_copy = pltpu.make_async_copy(alive_ref, loaded_alive_ref, sems.at[block // step + 1])
    for copy in [*copies, alive_copy, bins_copy]:
        copy.start()
    half = half_here()
    for channel in range(block):
        if channel % step == 0:
            copies[channel // step].wait()
        if channel == 0:
            alive_copy.wait()
        values = loaded_ref[channel].astype(F32)
        powers = jnp.mean(values * values, axis=-1, keepdims=True)
        values = values * (lax.rsqrt(powers + 1e-06) * loaded_alive_ref[channel].astype(F32))
        for tile in range(columns // LANES):
            scaled_ref[tile, channel * width : (channel + 1) * width, :] = values[:, tile * LANES : (tile + 1) * LANES]
    planes = keep_ref.shape[0] - 1
    firsts = first_ref.shape[0] - 1
    for plane in range(planes):
        sent = plane_of(scaled_ref, plane, block, 1 - half).astype(BF16)
        whole_ref[plane] = sent
        if plane < firsts:
            first_ref[plane] = sent
        else:
            second_ref[plane - firsts] = sent
        keep_ref[plane] = plane_of(scaled_ref, plane, block, half).astype(BF16).astype(F32)
    bins_copy.wait()
    bins = jnp.zeros((block, LANES), F32)
    for round_no in range(bins_ref.shape[0]):
        place = one_hot(block, LANES, -block * round_no, lambda ids: ids)
        bins = bins + jnp.dot(loaded_bins_ref[round_no].astype(F32).astype(BF16), place, preferred_element_type=F32)
    whole_ref[planes] = bins.astype(BF16)
    keep_ref[planes] = bins
    first_ref[firsts] = bins.astype(BF16)


def whiten(spectra, bins, alive, first_tiles):
    block, width, columns = spectra.shape
    planes = columns // 2 // LANES * width
    firsts = first_tiles * 2 * width

    def sent(count):
        return jax.ShapeDtypeStruct((count, block, LANES), BF16)

    return pl.pallas_call(
        whiten_kernel,
        out_shape=(
            sent(firsts + 1),
            sent(planes - firsts),
            sent(planes + 1),
            jax.ShapeDtypeStruct((planes + 1, block, LANES), F32),
        ),
        in_specs=[HBM, HBM, HBM],
        out_specs=(VMEM,) * 4,
        scratch_shapes=[
            pltpu.VMEM((columns // LANES, block * width, LANES), F32),
            pltpu.VMEM(spectra.shape, BF16),
            pltpu.VMEM(bins.shape, jnp.int32),
            pltpu.SMEM(alive.shape, jnp.int32),
            pltpu.SemaphoreType.DMA((block // 8 + 2,)),
        ],
        compiler_params=LARGE,
        name="whiten",
    )(spectra, bins, alive)


def hot_pairs(mine, theirs, round_no, block):
    pairs = block * block
    base = block * round_no
    rows = lax.broadcasted_iota(jnp.int32, (block, pairs), 0)
    columns = lax.broadcasted_iota(jnp.int32, (block, pairs), 1)
    by_second = jnp.dot(mine, one_hot(LANES, pairs, base, lambda ids: ids % block), preferred_element_type=F32)
    by_first = jnp.dot(theirs, one_hot(LANES, pairs, base, lambda ids: ids // block), preferred_element_type=F32)
    first = jnp.sum(jnp.where(rows == columns // block, by_second, 0.0), axis=0, keepdims=True)
    second = jnp.sum(jnp.where(rows == columns % block, by_first, 0.0), axis=0, keepdims=True)
    bin_ids = lax.broadcasted_iota(jnp.int32, (NB, pairs), 0).astype(F32).astype(BF16)
    one, zero = jnp.ones((NB, pairs), BF16), jnp.zeros((NB, pairs), BF16)
    hot_first = jnp.where(bin_ids == jnp.broadcast_to(first.astype(BF16), (NB, pairs)), one, zero)
    hot_second = jnp.where(bin_ids == jnp.broadcast_to(second.astype(BF16), (NB, pairs)), one, zero)
    return hot_first + hot_second, hot_first - hot_second


def products(keep_ref, gots, cross_ref, width, here):
    block = keep_ref.shape[1]

    def of_channel(channel, carry):
        ones = [
            jnp.broadcast_to(keep_ref[here + k, pl.ds(channel, 1), :], (ROWS, LANES)).astype(BF16)
            for k in range(2 * width)
        ]
        for number, (got_ref, there) in enumerate(gots):
            for start in range(0, block, ROWS):
                at = pl.ds(pl.multiple_of(channel * block + start, ROWS), ROWS)
                for some in range(width // SUMMED):
                    real, imag = None, None
                    for window in range(some * SUMMED, (some + 1) * SUMMED):
                        one_real, one_imag = ones[2 * window], ones[2 * window + 1]
                        two_real = got_ref[there + 2 * window, start : start + ROWS, :]
                        two_imag = got_ref[there + 2 * window + 1, start : start + ROWS, :]
                        more_real = one_real * two_real + one_imag * two_imag
                        more_imag = one_imag * two_real - one_real * two_imag
                        real = more_real if real is None else real + more_real
                        imag = more_imag if imag is None else imag + more_imag
                    lanes = slice(some % 2 * LANES, (some % 2 + 1) * LANES)
                    cross_ref[number, 0, some // 2, at, lanes] = real
                    cross_ref[number, 1, some // 2, at, lanes] = imag
        return carry

    lax.fori_loop(0, block, of_channel, 0, unroll=8 // len(gots))


def binned(hots_refs, cross_ref, part):
    total = None
    for number, hots_ref in enumerate(hots_refs):
        for some in range(cross_ref.shape[2]):
            more = jnp.dot(hots_ref[part], cross_ref[number, part, some], preferred_element_type=F32)
            total = more if total is None else total + more
    return total[:, :LANES] + total[:, LANES:]


def table_copies(table_ref, loaded_ref, sems, start):
    rows = loaded_ref.shape[1]
    half = half_here()
    return [
        pltpu.make_async_copy(table_ref.at[half, level, pl.ds(start, rows)], loaded_ref.at[level], sems.at[level])
        for level in range(2)
    ]


def lags_of(sums, loaded_ref):
    values = jnp.concatenate(sums, axis=1)
    high = values.astype(BF16)
    low = (values - high.astype(F32)).astype(BF16)
    result = jnp.dot(high, loaded_ref[0], preferred_element_type=F32)
    result = result + jnp.dot(low, loaded_ref[0], preferred_element_type=F32)
    return result + jnp.dot(high, loaded_ref[1], preferred_element_type=F32)


def stage_kernel(plan, *refs):
    refs = iter(refs)
    take = lambda count: [next(refs) for _ in range(count)]
    (keep_ref,), got_refs = take(1), take(plan["gots"])
    hots_refs, before_refs = take(plan["hots"]), take(len(plan["before"]))
    table_ref = next(refs) if plan["full"] else None
    lags_ref = next(refs) if plan["lags"] else None
    after_refs = take(len(plan["after"]))
    out_ref = next(refs) if plan["full"] else None
    hots_refs = hots_refs + take(len(plan["rounds"]))
    cross_ref = next(refs)
    width = plan["width"]
    if plan["full"]:
        loaded_ref, sums_ref, sems = take(3)
        copies = table_copies(table_ref, loaded_ref, sems, min(plan["full"]) * 2 * LANES)
        for copy in copies:
            copy.start()
    for round_no, got_ref, hots_ref in zip(plan["rounds"], got_refs, hots_refs):
        mine, theirs = keep_ref[keep_ref.shape[0] - 1].astype(BF16), got_ref[got_ref.shape[0] - 1]
        plus, minus = hot_pairs(mine, theirs, round_no, keep_ref.shape[1])
        hots_ref[0] = plus
        hots_ref[1] = minus
    places = {tile: ref for tile, ref in zip(plan["before"], before_refs)}
    for tile, starts in plan["jobs"]:
        products(keep_ref, list(zip(got_refs, starts)), cross_ref, width, tile * 2 * width)
        to = after_refs[plan["after"].index(tile)] if tile in plan["after"] else sums_ref.at[plan["full"].index(tile)]
        for part in range(2):
            sums = binned(hots_refs, cross_ref, part)
            to[part] = sums + places[tile][part] if tile in places else sums
        places[tile] = to
    if plan["full"]:
        sums = [places[tile][part] for tile in plan["full"] for part in range(2)]
        for copy in copies:
            copy.wait()
        lags = lags_of(sums, loaded_ref)
        if lags_ref is not None:
            lags = lags + lags_ref[...]
        out_ref[...] = lags.astype(out_ref.dtype)


def stage(width, keep, gots, hots, rounds, jobs, before, full=(), table=None, lags=None, lags_type=F32):
    block = keep.shape[1]
    pairs = block * block
    after = [tile for tile, _ in jobs if tile not in full]
    plan = {
        "width": width,
        "gots": len(gots),
        "hots": len(hots),
        "rounds": rounds,
        "jobs": jobs,
        "before": list(before),
        "after": after,
        "full": list(full),
        "lags": lags is not None,
    }
    out = [jax.ShapeDtypeStruct((2, NB, LANES), F32)] * len(after)
    scratch = [pltpu.VMEM((len(gots), 2, width // SUMMED // 2, pairs, 2 * LANES), BF16)]
    inputs = [keep, *gots, *hots, *before.values()]
    specs = [VMEM] * len(inputs)
    if full:
        inputs, specs = inputs + [table], specs + [HBM]
        out.append(jax.ShapeDtypeStruct((NB, LAGS), lags_type))
        scratch += [
            pltpu.VMEM((2, len(full) * 2 * LANES, LAGS), BF16),
            pltpu.VMEM((len(full), 2, NB, LANES), F32),
            pltpu.SemaphoreType.DMA((2,)),
        ]
    if lags is not None:
        inputs, specs = inputs + [lags], specs + [VMEM]
    out += [jax.ShapeDtypeStruct((2, NB, pairs), BF16)] * len(rounds)
    results = pl.pallas_call(
        functools.partial(stage_kernel, plan),
        out_shape=out,
        in_specs=specs,
        out_specs=[VMEM] * len(out),
        scratch_shapes=scratch,
        compiler_params=PARAMS,
        name="stage",
    )(*inputs)
    count = len(after)
    lags_out = results[count] if full else None
    return dict(zip(after, results)), list(results[count + bool(full) :]), lags_out


def sum_kernel(scaling, parts_ref, out_ref):
    total = parts_ref[0].astype(F32)
    for source in range(1, parts_ref.shape[0]):
        total = total + parts_ref[source].astype(F32)
    out_ref[...] = total * scaling


def summed(parts, scaling):
    return pl.pallas_call(
        functools.partial(sum_kernel, scaling),
        out_shape=jax.ShapeDtypeStruct(parts.shape[1:], F32),
        in_specs=[VMEM],
        out_specs=VMEM,
        compiler_params=PARAMS,
        name="summed",
    )(parts)


def build_table(freq_len):
    freq_ids = np.arange(freq_len).reshape(2, freq_len // 2 // LANES, 1, LANES)
    lag_ids = np.arange(LAGS) - LAGS // 2
    angles = (freq_ids[..., None] * lag_ids % NT) * (2.0 * math.pi / NT)
    weights = np.where(freq_ids == 0, 1.0, 2.0)[..., None]
    table = np.concatenate([weights * np.cos(angles), -weights * np.sin(angles)], axis=2)
    table = table.reshape(2, freq_len, LAGS).astype(np.float32)
    high = table.astype(BF16)
    return np.stack([high, (table - high.astype(np.float32)).astype(BF16)], axis=1)


def on_device(spectra, pair_bins, dead_mask):
    block, width, columns = spectra.shape
    freq_len = columns // 2
    groups = lax.axis_size("row") * lax.axis_size("col")
    table = jnp.asarray(build_table(freq_len))
    tile_planes = 2 * width

    def send(value, round_no):
        return swapped(value, round_no, groups)

    first, second, whole, keep = whiten(spectra, pair_bins, dead_mask, 2)
    core, across, far_first, near_first = send(whole, 0), send(whole, 3), send(first, 2), send(first, 1)
    far_second, near_second = send(second, 2), send(second, 1)
    work = functools.partial(stage, width, keep)
    jobs = [(tile, (tile * tile_planes,)) for tile in range(3)]
    sums, _, _ = work([core], [], [0], jobs, {})
    sums, _, _ = work([across], [], [3], jobs, sums)
    jobs = [(tile, (tile * tile_planes,) * 2) for tile in range(2)]
    _, hots, lags = work([far_first, near_first], [], [2, 1], jobs, {0: sums[0], 1: sums[1]}, (0, 1), table)
    _, _, lags = work([far_second, near_second], hots, [], [(2, (0, 0))], {2: sums[2]}, (2,), table, lags, BF16)
    mine = lax.all_to_all(lags.reshape(groups, NB // groups, LAGS), AXES, 0, 0, tiled=True)
    pairs = ROUNDS * block * block * groups // NB
    return summed(mine, 1.0 / (2.0 * math.sqrt(freq_len * width * pairs)))


def solution(mesh):
    return jax.shard_map(
        on_device,
        mesh=mesh,
        in_specs=(P(AXES, None, None), P(None, AXES, None), P(AXES)),
        out_specs=P(AXES, None),
        check_vma=False,
    )
```

```python
import functools
import math

import jax
import jax.numpy as jnp
import numpy as np
from jax import lax
from jax.experimental import pallas as pl
from jax.experimental.pallas import tpu as pltpu
from jax.sharding import PartitionSpec as P

NT = 1600
LAGS = 896
NB = 128
ROUNDS = 4
LANES = 128
ROWS = 16
STEP = 16
SUMMED = 2
AXES = ("row", "col")
F32 = jnp.float32
BF16 = jnp.bfloat16
VMEM = pl.BlockSpec(memory_space=pltpu.VMEM)
HBM = pl.BlockSpec(memory_space=pltpu.MemorySpace.HBM)
LARGE = pltpu.CompilerParams(vmem_limit_bytes=63488 * 2**10)
PARAMS = pltpu.CompilerParams(vmem_limit_bytes=48 * 2**20)


def parity_of(index):
    total = 0
    for bit in range(ROUNDS):
        total = total + ((index >> bit) & 1)
    return total % 2


def half_here():
    return parity_of(lax.axis_index("row") * lax.axis_size("col") + lax.axis_index("col"))


def swapped(value, stride, groups):
    mask = 2**stride
    return lax.ppermute(value, AXES, [(source, source ^ mask) for source in range(groups)])


def one_hot(rows, columns, row_offset, of_column):
    row_ids = lax.broadcasted_iota(jnp.int32, (rows, columns), 0)
    column_ids = lax.broadcasted_iota(jnp.int32, (rows, columns), 1)
    return (row_ids == row_offset + of_column(column_ids)).astype(BF16)


def plane_of(scaled_ref, plane, block, half):
    tiles, width = scaled_ref.shape[0] // 4, scaled_ref.shape[1] // block
    tile, window, part = plane // (2 * width), plane // 2 % width, plane % 2
    return scaled_ref[2 * tiles * part + tiles * half + tile, pl.ds(window, block, stride=width), :]


def whiten_kernel(spectra_ref, bins_ref, alive_ref, *refs):
    (first_ref, second_ref, whole_ref, keep_ref), refs = refs[:4], refs[4:]
    scaled_ref, loaded_ref, loaded_bins_ref, loaded_alive_ref, sent_ref, kept_ref, sems, out_sems = refs
    block, width, columns = spectra_ref.shape
    copies = [
        pltpu.make_async_copy(spectra_ref.at[pl.ds(at, STEP)], loaded_ref.at[pl.ds(at, STEP)], sems.at[at // STEP])
        for at in range(0, block, STEP)
    ]
    bins_copy = pltpu.make_async_copy(bins_ref, loaded_bins_ref, sems.at[block // STEP])
    alive_copy = pltpu.make_async_copy(alive_ref, loaded_alive_ref, sems.at[block // STEP + 1])
    for copy in [*copies, alive_copy, bins_copy]:
        copy.start()
    half = half_here()
    for channel in range(block):
        if channel % STEP == 0:
            copies[channel // STEP].wait()
        if channel == 0:
            alive_copy.wait()
        values = loaded_ref[channel].astype(F32)
        powers = jnp.mean(values * values, axis=-1, keepdims=True)
        values = values * (lax.rsqrt(powers + 1e-06) * loaded_alive_ref[channel].astype(F32))
        for tile in range(columns // LANES):
            scaled_ref[tile, channel * width : (channel + 1) * width, :] = values[:, tile * LANES : (tile + 1) * LANES]
    planes = sent_ref.shape[0] - 1
    firsts = first_ref.shape[0] - 1
    going = []

    def go(source, target):
        going.append(pltpu.make_async_copy(source, target, out_sems.at[len(going)]))
        going[-1].start()

    bins_copy.wait()
    bins = jnp.zeros((block, LANES), F32)
    for round_no in range(bins_ref.shape[0]):
        place = one_hot(block, LANES, -block * round_no, lambda ids: ids)
        bins = bins + jnp.dot(loaded_bins_ref[round_no].astype(F32).astype(BF16), place, preferred_element_type=F32)
    sent_ref[planes] = bins.astype(BF16)
    kept_ref[planes] = bins.astype(BF16)
    for plane in range(planes):
        sent_ref[plane] = plane_of(scaled_ref, plane, block, 1 - half).astype(BF16)
        if plane == firsts - 1:
            go(sent_ref.at[pl.ds(0, firsts)], first_ref.at[pl.ds(0, firsts)])
            go(sent_ref.at[pl.ds(planes, 1)], first_ref.at[pl.ds(firsts, 1)])
    go(sent_ref, whole_ref)
    go(sent_ref.at[pl.ds(firsts, planes - firsts)], second_ref)
    for plane in range(planes):
        kept_ref[plane] = plane_of(scaled_ref, plane, block, half).astype(BF16)
    go(kept_ref, keep_ref)
    for copy in going:
        copy.wait()


def whiten(spectra, bins, alive, first_tiles):
    block, width, columns = spectra.shape
    planes = columns // 2 // LANES * width
    firsts = first_tiles * 2 * width

    def sent(count):
        return jax.ShapeDtypeStruct((count, block, LANES), BF16)

    return pl.pallas_call(
        whiten_kernel,
        out_shape=(sent(firsts + 1), sent(planes - firsts), sent(planes + 1), sent(planes + 1)),
        in_specs=[HBM, HBM, HBM],
        out_specs=(HBM,) * 4,
        scratch_shapes=[
            pltpu.VMEM((columns // LANES, block * width, LANES), F32),
            pltpu.VMEM(spectra.shape, BF16),
            pltpu.VMEM(bins.shape, jnp.int32),
            pltpu.SMEM(alive.shape, jnp.int32),
            pltpu.VMEM((planes + 1, block, LANES), BF16),
            pltpu.VMEM((planes + 1, block, LANES), BF16),
            pltpu.SemaphoreType.DMA((block // STEP + 2,)),
            pltpu.SemaphoreType.DMA((5,)),
        ],
        compiler_params=LARGE,
        name="whiten",
    )(spectra, bins, alive)


def hot_pairs(mine, theirs, round_no, block):
    pairs = block * block
    base = block * round_no
    rows = lax.broadcasted_iota(jnp.int32, (block, pairs), 0)
    columns = lax.broadcasted_iota(jnp.int32, (block, pairs), 1)
    by_second = jnp.dot(mine, one_hot(LANES, pairs, base, lambda ids: ids % block), preferred_element_type=F32)
    by_first = jnp.dot(theirs, one_hot(LANES, pairs, base, lambda ids: ids // block), preferred_element_type=F32)
    first = jnp.sum(jnp.where(rows == columns // block, by_second, 0.0), axis=0, keepdims=True)
    second = jnp.sum(jnp.where(rows == columns % block, by_first, 0.0), axis=0, keepdims=True)
    bin_ids = lax.broadcasted_iota(jnp.int32, (NB, pairs), 0).astype(F32).astype(BF16)
    one, zero = jnp.ones((NB, pairs), BF16), jnp.zeros((NB, pairs), BF16)
    hot_first = jnp.where(bin_ids == jnp.broadcast_to(first.astype(BF16), (NB, pairs)), one, zero)
    hot_second = jnp.where(bin_ids == jnp.broadcast_to(second.astype(BF16), (NB, pairs)), one, zero)
    return hot_first + hot_second, hot_first - hot_second


def products(keep_ref, gots, cross_ref, width, here):
    block = keep_ref.shape[1]

    def of_channel(channel, carry):
        ones = [
            jnp.broadcast_to(keep_ref[here + k, pl.ds(channel, 1), :], (ROWS, LANES)).astype(BF16)
            for k in range(2 * width)
        ]
        for number, (got_ref, there) in enumerate(gots):
            for start in range(0, block, ROWS):
                at = pl.ds(pl.multiple_of(channel * block + start, ROWS), ROWS)
                for some in range(width // SUMMED):
                    real, imag = None, None
                    for window in range(some * SUMMED, (some + 1) * SUMMED):
                        one_real, one_imag = ones[2 * window], ones[2 * window + 1]
                        two_real = got_ref[there + 2 * window, start : start + ROWS, :]
                        two_imag = got_ref[there + 2 * window + 1, start : start + ROWS, :]
                        more_real = one_real * two_real + one_imag * two_imag
                        more_imag = one_imag * two_real - one_real * two_imag
                        real = more_real if real is None else real + more_real
                        imag = more_imag if imag is None else imag + more_imag
                    lanes = slice(some % 2 * LANES, (some % 2 + 1) * LANES)
                    cross_ref[number, 0, some // 2, at, lanes] = real
                    cross_ref[number, 1, some // 2, at, lanes] = imag
        return carry

    lax.fori_loop(0, block, of_channel, 0, unroll=8 // len(gots))


def binned(hots_refs, cross_ref, part):
    total = None
    for number, hots_ref in enumerate(hots_refs):
        for some in range(cross_ref.shape[2]):
            more = jnp.dot(hots_ref[part], cross_ref[number, part, some], preferred_element_type=F32)
            total = more if total is None else total + more
    return total[:, :LANES] + total[:, LANES:]


def table_copies(table_ref, loaded_ref, sems, start):
    rows = loaded_ref.shape[1]
    half = half_here()
    return [
        pltpu.make_async_copy(table_ref.at[half, level, pl.ds(start, rows)], loaded_ref.at[level], sems.at[level])
        for level in range(2)
    ]


def lags_of(sums, loaded_ref):
    values = jnp.concatenate(sums, axis=1)
    high = values.astype(BF16)
    low = (values - high.astype(F32)).astype(BF16)
    result = jnp.dot(high, loaded_ref[0], preferred_element_type=F32)
    result = result + jnp.dot(low, loaded_ref[0], preferred_element_type=F32)
    return result + jnp.dot(high, loaded_ref[1], preferred_element_type=F32)


def stage_kernel(plan, *refs):
    refs = iter(refs)
    take = lambda count: [next(refs) for _ in range(count)]
    (keep_ref,), got_refs = take(1), take(plan["gots"])
    hots_refs, before_refs = take(plan["hots"]), take(len(plan["before"]))
    table_ref = next(refs) if plan["full"] else None
    lags_ref = next(refs) if plan["lags"] else None
    after_refs = take(len(plan["after"]))
    out_ref = next(refs) if plan["full"] else None
    wide_ref = next(refs) if plan["widens"] else None
    hots_refs = hots_refs + take(len(plan["rounds"]))
    if plan["widens"]:
        wide_ref[...] = keep_ref[...].astype(F32)
        keep_ref = wide_ref
    cross_ref = next(refs)
    width = plan["width"]
    if plan["full"]:
        loaded_ref, sums_ref, sems = take(3)
        copies = table_copies(table_ref, loaded_ref, sems, min(plan["full"]) * 2 * LANES)
        for copy in copies:
            copy.start()
    for round_no, got_ref, hots_ref in zip(plan["rounds"], got_refs, hots_refs):
        mine, theirs = keep_ref[keep_ref.shape[0] - 1].astype(BF16), got_ref[got_ref.shape[0] - 1]
        plus, minus = hot_pairs(mine, theirs, round_no, keep_ref.shape[1])
        hots_ref[0] = plus
        hots_ref[1] = minus
    places = {tile: ref for tile, ref in zip(plan["before"], before_refs)}
    for tile, starts in plan["jobs"]:
        products(keep_ref, list(zip(got_refs, starts)), cross_ref, width, tile * 2 * width)
        to = after_refs[plan["after"].index(tile)] if tile in plan["after"] else sums_ref.at[plan["full"].index(tile)]
        for part in range(2):
            sums = binned(hots_refs, cross_ref, part)
            to[part] = sums + places[tile][part] if tile in places else sums
        places[tile] = to
    if plan["full"]:
        sums = [places[tile][part] for tile in plan["full"] for part in range(2)]
        for copy in copies:
            copy.wait()
        lags = lags_of(sums, loaded_ref)
        if lags_ref is not None:
            lags = lags + lags_ref[...]
        out_ref[...] = lags.astype(out_ref.dtype)


def stage(width, keep, gots, hots, rounds, jobs, before, full=(), table=None, lags=None, lags_type=F32, gives_hots=False):
    block = keep.shape[1]
    pairs = block * block
    after = [tile for tile, _ in jobs if tile not in full]
    plan = {
        "width": width,
        "gots": len(gots),
        "hots": len(hots),
        "rounds": rounds,
        "jobs": jobs,
        "before": list(before),
        "after": after,
        "full": list(full),
        "lags": lags is not None,
        "widens": keep.dtype != F32,
    }
    out = [jax.ShapeDtypeStruct((2, NB, LANES), F32)] * len(after)
    scratch = [pltpu.VMEM((len(gots), 2, width // SUMMED // 2, pairs, 2 * LANES), BF16)]
    inputs = [keep, *gots, *hots, *before.values()]
    specs = [VMEM] * len(inputs)
    if full:
        inputs, specs = inputs + [table], specs + [HBM]
        out.append(jax.ShapeDtypeStruct((NB, LAGS), lags_type))
        scratch += [
            pltpu.VMEM((2, len(full) * 2 * LANES, LAGS), BF16),
            pltpu.VMEM((len(full), 2, NB, LANES), F32),
            pltpu.SemaphoreType.DMA((2,)),
        ]
    if lags is not None:
        inputs, specs = inputs + [lags], specs + [VMEM]
    if keep.dtype != F32:
        out.append(jax.ShapeDtypeStruct(keep.shape, F32))
    if gives_hots:
        out += [jax.ShapeDtypeStruct((2, NB, pairs), BF16)] * len(rounds)
    else:
        scratch = [pltpu.VMEM((2, NB, pairs), BF16)] * len(rounds) + scratch
    results = pl.pallas_call(
        functools.partial(stage_kernel, plan),
        out_shape=out,
        in_specs=specs,
        out_specs=[VMEM] * len(out),
        scratch_shapes=scratch,
        compiler_params=PARAMS,
        name="stage",
    )(*inputs)
    count = len(after)
    lags_out = results[count] if full else None
    return dict(zip(after, results)), list(results[count + bool(full) :]), lags_out


def sum_kernel(scaling, parts_ref, out_ref):
    total = parts_ref[0].astype(F32)
    for source in range(1, parts_ref.shape[0]):
        total = total + parts_ref[source].astype(F32)
    out_ref[...] = total * scaling


def summed(parts, scaling):
    return pl.pallas_call(
        functools.partial(sum_kernel, scaling),
        out_shape=jax.ShapeDtypeStruct(parts.shape[1:], F32),
        in_specs=[VMEM],
        out_specs=VMEM,
        compiler_params=PARAMS,
        name="summed",
    )(parts)


def build_table(freq_len):
    freq_ids = np.arange(freq_len).reshape(2, freq_len // 2 // LANES, 1, LANES)
    lag_ids = np.arange(LAGS) - LAGS // 2
    angles = (freq_ids[..., None] * lag_ids % NT) * (2.0 * math.pi / NT)
    weights = np.where(freq_ids == 0, 1.0, 2.0)[..., None]
    table = np.concatenate([weights * np.cos(angles), -weights * np.sin(angles)], axis=2)
    table = table.reshape(2, freq_len, LAGS).astype(np.float32)
    high = table.astype(BF16)
    return np.stack([high, (table - high.astype(np.float32)).astype(BF16)], axis=1)


def on_device(spectra, pair_bins, dead_mask):
    block, width, columns = spectra.shape
    freq_len = columns // 2
    groups = lax.axis_size("row") * lax.axis_size("col")
    table = jnp.asarray(build_table(freq_len))
    tile_planes = 2 * width

    def send(value, round_no):
        return swapped(value, round_no, groups)

    first, second, whole, keep = whiten(spectra, pair_bins, dead_mask, 2)
    core, far_first, near_first = send(whole, 0), send(first, 2), send(first, 1)
    across_first, across_second = send(first, 3), send(second, 3)

    def planes(tiles, gots=1):
        return [(tile, ((tile - tiles[0]) * tile_planes,) * gots) for tile in tiles]

    sums, (keep,), _ = stage(width, keep, [core], [], [0], planes((0, 1, 2)), {})
    work = functools.partial(stage, width, keep)
    low, across_hots, _ = work([across_first], [], [3], planes((0, 1)), {0: sums[0], 1: sums[1]}, gives_hots=True)
    high, _, _ = work([across_second], across_hots, [], planes((2,)), {2: sums[2]})
    second, low, high = lax.optimization_barrier((second, low, high))
    far_second, near_second = send(second, 2), send(second, 1)
    _, hots, lags = work([far_first, near_first], [], [2, 1], planes((0, 1), 2), low, (0, 1), table, gives_hots=True)
    _, _, lags = work([far_second, near_second], hots, [], planes((2,), 2), high, (2,), table, lags, BF16)
    mine = lax.all_to_all(lags.reshape(groups, NB // groups, LAGS), AXES, 0, 0, tiled=True)
    pairs = ROUNDS * block * block * groups // NB
    return summed(mine, 1.0 / (2.0 * math.sqrt(freq_len * width * pairs)))


def solution(mesh):
    return jax.shard_map(
        on_device,
        mesh=mesh,
        in_specs=(P(AXES, None, None), P(None, AXES, None), P(AXES)),
        out_specs=P(AXES, None),
        check_vma=False,
    )
```

```python
import functools
import math

import jax
import jax.numpy as jnp
import numpy as np
from jax import lax
from jax.experimental import pallas as pl
from jax.experimental.pallas import tpu as pltpu
from jax.sharding import PartitionSpec as P

NT = 1600
LAGS = 896
NB = 128
ROUNDS = 4
LANES = 128
ROWS = 16
STEP = 16
SUMMED = 2
AXES = ("row", "col")
F32 = jnp.float32
BF16 = jnp.bfloat16
VMEM = pl.BlockSpec(memory_space=pltpu.VMEM)
HBM = pl.BlockSpec(memory_space=pltpu.MemorySpace.HBM)
LARGE = pltpu.CompilerParams(vmem_limit_bytes=63488 * 2**10)
PARAMS = pltpu.CompilerParams(vmem_limit_bytes=48 * 2**20)


def parity_of(index):
    total = 0
    for bit in range(ROUNDS):
        total = total + ((index >> bit) & 1)
    return total % 2


def half_here():
    return parity_of(lax.axis_index("row") * lax.axis_size("col") + lax.axis_index("col"))


def swapped(value, stride, groups):
    mask = 2**stride
    return lax.ppermute(value, AXES, [(source, source ^ mask) for source in range(groups)])


def one_hot(rows, columns, row_offset, of_column):
    row_ids = lax.broadcasted_iota(jnp.int32, (rows, columns), 0)
    column_ids = lax.broadcasted_iota(jnp.int32, (rows, columns), 1)
    return (row_ids == row_offset + of_column(column_ids)).astype(BF16)


def plane_of(scaled_ref, plane, block, half):
    tiles, width = scaled_ref.shape[0] // 4, scaled_ref.shape[1] // block
    tile, window, part = plane // (2 * width), plane // 2 % width, plane % 2
    return scaled_ref[2 * tiles * part + tiles * half + tile, pl.ds(window, block, stride=width), :]


def whiten_kernel(spectra_ref, bins_ref, alive_ref, *refs):
    (first_ref, second_ref, whole_ref, keep_ref), refs = refs[:4], refs[4:]
    scaled_ref, loaded_ref, loaded_bins_ref, loaded_alive_ref, sent_ref, kept_ref, sems, out_sems = refs
    block, width, columns = spectra_ref.shape
    copies = [
        pltpu.make_async_copy(spectra_ref.at[pl.ds(at, STEP)], loaded_ref.at[pl.ds(at, STEP)], sems.at[at // STEP])
        for at in range(0, block, STEP)
    ]
    bins_copy = pltpu.make_async_copy(bins_ref, loaded_bins_ref, sems.at[block // STEP])
    alive_copy = pltpu.make_async_copy(alive_ref, loaded_alive_ref, sems.at[block // STEP + 1])
    for copy in [*copies, alive_copy, bins_copy]:
        copy.start()
    half = half_here()
    for channel in range(block):
        if channel % STEP == 0:
            copies[channel // STEP].wait()
        if channel == 0:
            alive_copy.wait()
        values = loaded_ref[channel].astype(F32)
        powers = jnp.mean(values * values, axis=-1, keepdims=True)
        values = values * (lax.rsqrt(powers + 1e-06) * loaded_alive_ref[channel].astype(F32))
        for tile in range(columns // LANES):
            scaled_ref[tile, channel * width : (channel + 1) * width, :] = values[:, tile * LANES : (tile + 1) * LANES]
    planes = sent_ref.shape[0] - 1
    firsts = first_ref.shape[0] - 1
    going = []

    def go(source, target):
        going.append(pltpu.make_async_copy(source, target, out_sems.at[len(going)]))
        going[-1].start()

    bins_copy.wait()
    bins = jnp.zeros((block, LANES), F32)
    for round_no in range(bins_ref.shape[0]):
        place = one_hot(block, LANES, -block * round_no, lambda ids: ids)
        bins = bins + jnp.dot(loaded_bins_ref[round_no].astype(F32).astype(BF16), place, preferred_element_type=F32)
    sent_ref[planes] = bins.astype(BF16)
    kept_ref[planes] = bins.astype(BF16)
    for plane in range(planes):
        sent_ref[plane] = plane_of(scaled_ref, plane, block, 1 - half).astype(BF16)
        if plane == firsts - 1:
            go(sent_ref.at[pl.ds(0, firsts)], first_ref.at[pl.ds(0, firsts)])
            go(sent_ref.at[pl.ds(planes, 1)], first_ref.at[pl.ds(firsts, 1)])
    go(sent_ref, whole_ref)
    go(sent_ref.at[pl.ds(firsts, planes - firsts)], second_ref)
    for plane in range(planes):
        kept_ref[plane] = plane_of(scaled_ref, plane, block, half).astype(BF16)
    go(kept_ref, keep_ref)
    for copy in going:
        copy.wait()


def whiten(spectra, bins, alive, first_tiles):
    block, width, columns = spectra.shape
    planes = columns // 2 // LANES * width
    firsts = first_tiles * 2 * width

    def sent(count):
        return jax.ShapeDtypeStruct((count, block, LANES), BF16)

    return pl.pallas_call(
        whiten_kernel,
        out_shape=(sent(firsts + 1), sent(planes - firsts), sent(planes + 1), sent(planes + 1)),
        in_specs=[HBM, HBM, HBM],
        out_specs=(HBM,) * 4,
        scratch_shapes=[
            pltpu.VMEM((columns // LANES, block * width, LANES), F32),
            pltpu.VMEM(spectra.shape, BF16),
            pltpu.VMEM(bins.shape, jnp.int32),
            pltpu.SMEM(alive.shape, jnp.int32),
            pltpu.VMEM((planes + 1, block, LANES), BF16),
            pltpu.VMEM((planes + 1, block, LANES), BF16),
            pltpu.SemaphoreType.DMA((block // STEP + 2,)),
            pltpu.SemaphoreType.DMA((5,)),
        ],
        compiler_params=LARGE,
        name="whiten",
    )(spectra, bins, alive)


def hot_pairs(mine, theirs, round_no, block):
    pairs = block * block
    base = block * round_no
    rows = lax.broadcasted_iota(jnp.int32, (block, pairs), 0)
    columns = lax.broadcasted_iota(jnp.int32, (block, pairs), 1)
    by_second = jnp.dot(mine, one_hot(LANES, pairs, base, lambda ids: ids % block), preferred_element_type=F32)
    by_first = jnp.dot(theirs, one_hot(LANES, pairs, base, lambda ids: ids // block), preferred_element_type=F32)
    first = jnp.sum(jnp.where(rows == columns // block, by_second, 0.0), axis=0, keepdims=True)
    second = jnp.sum(jnp.where(rows == columns % block, by_first, 0.0), axis=0, keepdims=True)
    bin_ids = lax.broadcasted_iota(jnp.int32, (NB, pairs), 0).astype(F32).astype(BF16)
    one, zero = jnp.ones((NB, pairs), BF16), jnp.zeros((NB, pairs), BF16)
    hot_first = jnp.where(bin_ids == jnp.broadcast_to(first.astype(BF16), (NB, pairs)), one, zero)
    hot_second = jnp.where(bin_ids == jnp.broadcast_to(second.astype(BF16), (NB, pairs)), one, zero)
    return hot_first + hot_second, hot_first - hot_second


def products(keep_ref, gots, cross_ref, width, summed, here):
    block = keep_ref.shape[1]

    def of_channel(channel, carry):
        ones = [
            jnp.broadcast_to(keep_ref[here + k, pl.ds(channel, 1), :], (ROWS, LANES)).astype(BF16)
            for k in range(2 * width)
        ]
        for number, (got_ref, there) in enumerate(gots):
            for start in range(0, block, ROWS):
                at = pl.ds(pl.multiple_of(channel * block + start, ROWS), ROWS)
                for some in range(width // summed):
                    real, imag = None, None
                    for window in range(some * summed, (some + 1) * summed):
                        one_real, one_imag = ones[2 * window], ones[2 * window + 1]
                        two_real = got_ref[there + 2 * window, start : start + ROWS, :]
                        two_imag = got_ref[there + 2 * window + 1, start : start + ROWS, :]
                        more_real = one_real * two_real + one_imag * two_imag
                        more_imag = one_imag * two_real - one_real * two_imag
                        real = more_real if real is None else real + more_real
                        imag = more_imag if imag is None else imag + more_imag
                    lanes = slice(some % 2 * LANES, (some % 2 + 1) * LANES)
                    cross_ref[number, 0, some // 2, at, lanes] = real
                    cross_ref[number, 1, some // 2, at, lanes] = imag
        return carry

    lax.fori_loop(0, block, of_channel, 0, unroll=16 // len(gots))


def binned(hots_refs, cross_ref, part):
    total = None
    for number, hots_ref in enumerate(hots_refs):
        for some in range(cross_ref.shape[2]):
            more = jnp.dot(hots_ref[part], cross_ref[number, part, some], preferred_element_type=F32)
            total = more if total is None else total + more
    return total[:, :LANES] + total[:, LANES:]


def table_copies(table_ref, loaded_ref, sems, start):
    rows = loaded_ref.shape[1]
    half = half_here()
    return [
        pltpu.make_async_copy(table_ref.at[half, level, pl.ds(start, rows)], loaded_ref.at[level], sems.at[level])
        for level in range(2)
    ]


def lags_of(sums, loaded_ref):
    values = jnp.concatenate(sums, axis=1)
    high = values.astype(BF16)
    low = (values - high.astype(F32)).astype(BF16)
    result = jnp.dot(high, loaded_ref[0], preferred_element_type=F32)
    result = result + jnp.dot(low, loaded_ref[0], preferred_element_type=F32)
    return result + jnp.dot(high, loaded_ref[1], preferred_element_type=F32)


def stage_kernel(plan, *refs):
    refs = iter(refs)
    take = lambda count: [next(refs) for _ in range(count)]
    (keep_ref,), got_refs = take(1), take(plan["gots"])
    hots_refs, before_refs = take(plan["hots"]), take(len(plan["before"]))
    table_ref = next(refs) if plan["full"] else None
    lags_ref = next(refs) if plan["lags"] else None
    after_refs = take(len(plan["after"]))
    out_ref = next(refs) if plan["full"] else None
    wide_ref = next(refs) if plan["widens"] else None
    hots_refs = hots_refs + take(len(plan["rounds"]))
    if plan["widens"]:
        wide_ref[...] = keep_ref[...].astype(F32)
        keep_ref = wide_ref
    cross_ref = next(refs)
    width = plan["width"]
    if plan["full"]:
        loaded_ref, sums_ref, sems = take(3)
        copies = table_copies(table_ref, loaded_ref, sems, min(plan["full"]) * 2 * LANES)
        for copy in copies:
            copy.start()
    for round_no, got_ref, hots_ref in zip(plan["rounds"], got_refs, hots_refs):
        mine, theirs = keep_ref[keep_ref.shape[0] - 1].astype(BF16), got_ref[got_ref.shape[0] - 1]
        plus, minus = hot_pairs(mine, theirs, round_no, keep_ref.shape[1])
        hots_ref[0] = plus
        hots_ref[1] = minus
    places = {tile: ref for tile, ref in zip(plan["before"], before_refs)}
    for tile, starts in plan["jobs"]:
        products(keep_ref, list(zip(got_refs, starts)), cross_ref, width, plan["summed"], tile * 2 * width)
        to = after_refs[plan["after"].index(tile)] if tile in plan["after"] else sums_ref.at[plan["full"].index(tile)]
        for part in range(2):
            sums = binned(hots_refs, cross_ref, part)
            to[part] = sums + places[tile][part] if tile in places else sums
        places[tile] = to
    if plan["full"]:
        sums = [places[tile][part] for tile in plan["full"] for part in range(2)]
        for copy in copies:
            copy.wait()
        lags = lags_of(sums, loaded_ref)
        if lags_ref is not None:
            lags = lags + lags_ref[...]
        out_ref[...] = lags.astype(out_ref.dtype)


def stage(width, keep, gots, hots, rounds, jobs, before, full=(), table=None, lags=None, lags_type=F32, gives_hots=False, summed=SUMMED):
    block = keep.shape[1]
    pairs = block * block
    after = [tile for tile, _ in jobs if tile not in full]
    plan = {
        "width": width,
        "gots": len(gots),
        "hots": len(hots),
        "rounds": rounds,
        "jobs": jobs,
        "before": list(before),
        "after": after,
        "full": list(full),
        "lags": lags is not None,
        "summed": summed,
        "widens": keep.dtype != F32,
    }
    out = [jax.ShapeDtypeStruct((2, NB, LANES), F32)] * len(after)
    scratch = [pltpu.VMEM((len(gots), 2, width // summed // 2, pairs, 2 * LANES), BF16)]
    inputs = [keep, *gots, *hots, *before.values()]
    specs = [VMEM] * len(inputs)
    if full:
        inputs, specs = inputs + [table], specs + [HBM]
        out.append(jax.ShapeDtypeStruct((NB, LAGS), lags_type))
        scratch += [
            pltpu.VMEM((2, len(full) * 2 * LANES, LAGS), BF16),
            pltpu.VMEM((len(full), 2, NB, LANES), F32),
            pltpu.SemaphoreType.DMA((2,)),
        ]
    if lags is not None:
        inputs, specs = inputs + [lags], specs + [VMEM]
    if keep.dtype != F32:
        out.append(jax.ShapeDtypeStruct(keep.shape, F32))
    if gives_hots:
        out += [jax.ShapeDtypeStruct((2, NB, pairs), BF16)] * len(rounds)
    else:
        scratch = [pltpu.VMEM((2, NB, pairs), BF16)] * len(rounds) + scratch
    results = pl.pallas_call(
        functools.partial(stage_kernel, plan),
        out_shape=out,
        in_specs=specs,
        out_specs=[VMEM] * len(out),
        scratch_shapes=scratch,
        compiler_params=PARAMS,
        name="stage",
    )(*inputs)
    count = len(after)
    lags_out = results[count] if full else None
    return dict(zip(after, results)), list(results[count + bool(full) :]), lags_out


def sum_kernel(scaling, parts_ref, out_ref):
    total = parts_ref[0].astype(F32)
    for source in range(1, parts_ref.shape[0]):
        total = total + parts_ref[source].astype(F32)
    out_ref[...] = total * scaling


def summed(parts, scaling):
    return pl.pallas_call(
        functools.partial(sum_kernel, scaling),
        out_shape=jax.ShapeDtypeStruct(parts.shape[1:], F32),
        in_specs=[VMEM],
        out_specs=VMEM,
        compiler_params=PARAMS,
        name="summed",
    )(parts)


def build_table(freq_len):
    freq_ids = np.arange(freq_len).reshape(2, freq_len // 2 // LANES, 1, LANES)
    lag_ids = np.arange(LAGS) - LAGS // 2
    angles = (freq_ids[..., None] * lag_ids % NT) * (2.0 * math.pi / NT)
    weights = np.where(freq_ids == 0, 1.0, 2.0)[..., None]
    table = np.concatenate([weights * np.cos(angles), -weights * np.sin(angles)], axis=2)
    table = table.reshape(2, freq_len, LAGS).astype(np.float32)
    high = table.astype(BF16)
    return np.stack([high, (table - high.astype(np.float32)).astype(BF16)], axis=1)


def on_device(spectra, pair_bins, dead_mask):
    block, width, columns = spectra.shape
    freq_len = columns // 2
    groups = lax.axis_size("row") * lax.axis_size("col")
    table = jnp.asarray(build_table(freq_len))
    tile_planes = 2 * width

    def send(value, round_no):
        return swapped(value, round_no, groups)

    first, second, whole, keep = whiten(spectra, pair_bins, dead_mask, 2)
    core, far_first = send(whole, 0), send(first, 2)
    core, to_near = lax.optimization_barrier((core, first))
    near_first = send(to_near, 1)
    across_first, across_second = send(first, 3), send(second, 3)

    def planes(tiles, gots=1):
        return [(tile, ((tile - tiles[0]) * tile_planes,) * gots) for tile in tiles]

    sums, (keep,), _ = stage(width, keep, [core], [], [0], planes((0, 1, 2)), {})
    work = functools.partial(stage, width, keep)
    low, across_hots, _ = work([across_first], [], [3], planes((0, 1)), {0: sums[0], 1: sums[1]}, gives_hots=True)
    high, _, _ = work([across_second], across_hots, [], planes((2,)), {2: sums[2]})
    second, low, high = lax.optimization_barrier((second, low, high))
    far_second, near_second = send(second, 2), send(second, 1)
    _, hots, lags = work([far_first, near_first], [], [2, 1], planes((0, 1), 2), low, (0, 1), table, gives_hots=True)
    _, _, lags = work([far_second, near_second], hots, [], planes((2,), 2), high, (2,), table, lags, BF16, summed=2 * SUMMED)
    mine = lax.all_to_all(lags.reshape(groups, NB // groups, LAGS), AXES, 0, 0, tiled=True)
    pairs = ROUNDS * block * block * groups // NB
    return summed(mine, 1.0 / (2.0 * math.sqrt(freq_len * width * pairs)))


def solution(mesh):
    return jax.shard_map(
        on_device,
        mesh=mesh,
        in_specs=(P(AXES, None, None), P(None, AXES, None), P(AXES)),
        out_specs=P(AXES, None),
        check_vma=False,
    )
```

```python
import functools
import math

import jax
import jax.numpy as jnp
import numpy as np
from jax import lax
from jax.experimental import pallas as pl
from jax.experimental.pallas import tpu as pltpu
from jax.sharding import PartitionSpec as P

NT = 1600
LAGS = 896
NB = 128
ROUNDS = 4
LANES = 128
ROWS = 16
STEP = 16
SUMMED = 2
AXES = ("row", "col")
F32 = jnp.float32
BF16 = jnp.bfloat16
VMEM = pl.BlockSpec(memory_space=pltpu.VMEM)
HBM = pl.BlockSpec(memory_space=pltpu.MemorySpace.HBM)
LARGE = pltpu.CompilerParams(vmem_limit_bytes=63488 * 2**10)
PARAMS = pltpu.CompilerParams(vmem_limit_bytes=48 * 2**20)


def parity_of(index):
    total = 0
    for bit in range(ROUNDS):
        total = total + ((index >> bit) & 1)
    return total % 2


def half_here():
    return parity_of(lax.axis_index("row") * lax.axis_size("col") + lax.axis_index("col"))


def swapped(value, stride, groups):
    mask = 2**stride
    return lax.ppermute(value, AXES, [(source, source ^ mask) for source in range(groups)])


def one_hot(rows, columns, row_offset, of_column):
    row_ids = lax.broadcasted_iota(jnp.int32, (rows, columns), 0)
    column_ids = lax.broadcasted_iota(jnp.int32, (rows, columns), 1)
    return (row_ids == row_offset + of_column(column_ids)).astype(BF16)


def plane_of(scaled_ref, plane, block, half):
    tiles, width = scaled_ref.shape[0] // 4, scaled_ref.shape[1] // block
    tile, window, part = plane // (2 * width), plane // 2 % width, plane % 2
    return scaled_ref[2 * tiles * part + tiles * half + tile, pl.ds(window, block, stride=width), :]


def whiten_kernel(spectra_ref, bins_ref, alive_ref, *refs):
    (first_ref, second_ref, whole_ref, keep_ref), refs = refs[:4], refs[4:]
    scaled_ref, loaded_ref, loaded_bins_ref, loaded_alive_ref, sent_ref, kept_ref, sems, out_sems = refs
    block, width, columns = spectra_ref.shape
    copies = [
        pltpu.make_async_copy(spectra_ref.at[pl.ds(at, STEP)], loaded_ref.at[pl.ds(at, STEP)], sems.at[at // STEP])
        for at in range(0, block, STEP)
    ]
    bins_copy = pltpu.make_async_copy(bins_ref, loaded_bins_ref, sems.at[block // STEP])
    alive_copy = pltpu.make_async_copy(alive_ref, loaded_alive_ref, sems.at[block // STEP + 1])
    for copy in [bins_copy, alive_copy, *copies]:
        copy.start()
    half = half_here()
    planes = sent_ref.shape[0] - 1
    firsts = first_ref.shape[0] - 1
    bins_copy.wait()
    bins = jnp.zeros((block, LANES), F32)
    for round_no in range(bins_ref.shape[0]):
        place = one_hot(block, LANES, -block * round_no, lambda ids: ids)
        bins = bins + jnp.dot(loaded_bins_ref[round_no].astype(F32).astype(BF16), place, preferred_element_type=F32)
    sent_ref[planes] = bins.astype(BF16)
    kept_ref[planes] = bins.astype(BF16)
    for channel in range(block):
        if channel % STEP == 0:
            copies[channel // STEP].wait()
        if channel == 0:
            alive_copy.wait()
        values = loaded_ref[channel].astype(F32)
        powers = jnp.mean(values * values, axis=-1, keepdims=True)
        values = values * (lax.rsqrt(powers + 1e-06) * loaded_alive_ref[channel].astype(F32))
        for tile in range(columns // LANES):
            scaled_ref[tile, channel * width : (channel + 1) * width, :] = values[:, tile * LANES : (tile + 1) * LANES]
    going = []

    def go(source, target):
        going.append(pltpu.make_async_copy(source, target, out_sems.at[len(going)]))
        going[-1].start()

    for plane in range(planes):
        sent_ref[plane] = plane_of(scaled_ref, plane, block, 1 - half).astype(BF16)
        if plane == firsts - 1:
            go(sent_ref.at[pl.ds(0, firsts)], first_ref.at[pl.ds(0, firsts)])
            go(sent_ref.at[pl.ds(planes, 1)], first_ref.at[pl.ds(firsts, 1)])
    go(sent_ref, whole_ref)
    go(sent_ref.at[pl.ds(firsts, planes - firsts)], second_ref)
    for plane in range(planes):
        kept_ref[plane] = plane_of(scaled_ref, plane, block, half).astype(BF16)
    go(kept_ref, keep_ref)
    for copy in going:
        copy.wait()


def whiten(spectra, bins, alive, first_tiles):
    block, width, columns = spectra.shape
    planes = columns // 2 // LANES * width
    firsts = first_tiles * 2 * width

    def sent(count):
        return jax.ShapeDtypeStruct((count, block, LANES), BF16)

    return pl.pallas_call(
        whiten_kernel,
        out_shape=(sent(firsts + 1), sent(planes - firsts), sent(planes + 1), sent(planes + 1)),
        in_specs=[HBM, HBM, HBM],
        out_specs=(HBM,) * 4,
        scratch_shapes=[
            pltpu.VMEM((columns // LANES, block * width, LANES), F32),
            pltpu.VMEM(spectra.shape, BF16),
            pltpu.VMEM(bins.shape, jnp.int32),
            pltpu.SMEM(alive.shape, jnp.int32),
            pltpu.VMEM((planes + 1, block, LANES), BF16),
            pltpu.VMEM((planes + 1, block, LANES), BF16),
            pltpu.SemaphoreType.DMA((block // STEP + 2,)),
            pltpu.SemaphoreType.DMA((5,)),
        ],
        compiler_params=LARGE,
        name="whiten",
    )(spectra, bins, alive)


def hot_pairs(mine, theirs, round_no, block):
    pairs = block * block
    base = block * round_no
    rows = lax.broadcasted_iota(jnp.int32, (block, pairs), 0)
    columns = lax.broadcasted_iota(jnp.int32, (block, pairs), 1)
    by_second = jnp.dot(mine, one_hot(LANES, pairs, base, lambda ids: ids % block), preferred_element_type=F32)
    by_first = jnp.dot(theirs, one_hot(LANES, pairs, base, lambda ids: ids // block), preferred_element_type=F32)
    first = jnp.sum(jnp.where(rows == columns // block, by_second, 0.0), axis=0, keepdims=True)
    second = jnp.sum(jnp.where(rows == columns % block, by_first, 0.0), axis=0, keepdims=True)
    bin_ids = lax.broadcasted_iota(jnp.int32, (NB, pairs), 0).astype(F32).astype(BF16)
    one, zero = jnp.ones((NB, pairs), BF16), jnp.zeros((NB, pairs), BF16)
    hot_first = jnp.where(bin_ids == jnp.broadcast_to(first.astype(BF16), (NB, pairs)), one, zero)
    hot_second = jnp.where(bin_ids == jnp.broadcast_to(second.astype(BF16), (NB, pairs)), one, zero)
    return hot_first + hot_second, hot_first - hot_second


def products(keep_ref, gots, cross_ref, width, summed, here):
    block = keep_ref.shape[1]

    def of_channel(channel, carry):
        for some in range(width // summed):
            sums = {}
            for window in range(some * summed, (some + 1) * summed):
                one_real, one_imag = [
                    jnp.broadcast_to(keep_ref[here + 2 * window + k, pl.ds(channel, 1), :], (ROWS, LANES)).astype(BF16)
                    for k in range(2)
                ]
                for number, (got_ref, there) in enumerate(gots):
                    for start in range(0, block, ROWS):
                        two_real = got_ref[there + 2 * window, start : start + ROWS, :]
                        two_imag = got_ref[there + 2 * window + 1, start : start + ROWS, :]
                        real = one_real * two_real + one_imag * two_imag
                        imag = one_imag * two_real - one_real * two_imag
                        old = sums.get((number, start))
                        sums[number, start] = (real, imag) if old is None else (old[0] + real, old[1] + imag)
            lanes = slice(some % 2 * LANES, (some % 2 + 1) * LANES)
            for (number, start), pair in sums.items():
                at = pl.ds(pl.multiple_of(channel * block + start, ROWS), ROWS)
                for part in range(2):
                    cross_ref[number, part, some // 2, at, lanes] = pair[part]
        return carry

    lax.fori_loop(0, block, of_channel, 0, unroll=8 // len(gots))


def binned(hots_refs, cross_ref, part):
    total = None
    for number, hots_ref in enumerate(hots_refs):
        for some in range(cross_ref.shape[2]):
            more = jnp.dot(hots_ref[part], cross_ref[number, part, some], preferred_element_type=F32)
            total = more if total is None else total + more
    return total[:, :LANES] + total[:, LANES:]


def table_copies(table_ref, loaded_ref, sems, start):
    rows = loaded_ref.shape[1]
    half = half_here()
    return [
        pltpu.make_async_copy(table_ref.at[half, level, pl.ds(start, rows)], loaded_ref.at[level], sems.at[level])
        for level in range(2)
    ]


def lags_of(sums, loaded_ref):
    values = jnp.concatenate(sums, axis=1)
    high = values.astype(BF16)
    low = (values - high.astype(F32)).astype(BF16)
    result = jnp.dot(high, loaded_ref[0], preferred_element_type=F32)
    result = result + jnp.dot(low, loaded_ref[0], preferred_element_type=F32)
    return result + jnp.dot(high, loaded_ref[1], preferred_element_type=F32)


def stage_kernel(plan, *refs):
    refs = iter(refs)
    take = lambda count: [next(refs) for _ in range(count)]
    (keep_ref,), got_refs = take(1), take(plan["gots"])
    hots_refs, before_refs = take(plan["hots"]), take(len(plan["before"]))
    table_ref = next(refs) if plan["full"] else None
    lags_ref = next(refs) if plan["lags"] else None
    after_refs = take(len(plan["after"]))
    out_ref = next(refs) if plan["full"] else None
    wide_ref = next(refs) if plan["widens"] else None
    hots_refs = hots_refs + take(len(plan["rounds"]))
    if plan["widens"]:
        wide_ref[...] = keep_ref[...].astype(F32)
        keep_ref = wide_ref
    cross_ref = next(refs)
    width = plan["width"]
    if plan["full"]:
        loaded_ref, sums_ref, sems = take(3)
        copies = table_copies(table_ref, loaded_ref, sems, min(plan["full"]) * 2 * LANES)
        for copy in copies:
            copy.start()
    for round_no, got_ref, hots_ref in zip(plan["rounds"], got_refs, hots_refs):
        mine, theirs = keep_ref[keep_ref.shape[0] - 1].astype(BF16), got_ref[got_ref.shape[0] - 1]
        plus, minus = hot_pairs(mine, theirs, round_no, keep_ref.shape[1])
        hots_ref[0] = plus
        hots_ref[1] = minus
    places = {tile: ref for tile, ref in zip(plan["before"], before_refs)}
    for tile, starts in plan["jobs"]:
        products(keep_ref, list(zip(got_refs, starts)), cross_ref, width, plan["summed"], tile * 2 * width)
        to = after_refs[plan["after"].index(tile)] if tile in plan["after"] else sums_ref.at[plan["full"].index(tile)]
        for part in range(2):
            sums = binned(hots_refs, cross_ref, part)
            to[part] = sums + places[tile][part] if tile in places else sums
        places[tile] = to
    if plan["full"]:
        sums = [places[tile][part] for tile in plan["full"] for part in range(2)]
        for copy in copies:
            copy.wait()
        lags = lags_of(sums, loaded_ref)
        if lags_ref is not None:
            lags = lags + lags_ref[...]
        out_ref[...] = lags.astype(out_ref.dtype)


def stage(width, keep, gots, hots, rounds, jobs, before, full=(), table=None, lags=None, lags_type=F32, gives_hots=False, summed=SUMMED):
    block = keep.shape[1]
    pairs = block * block
    after = [tile for tile, _ in jobs if tile not in full]
    plan = {
        "width": width,
        "gots": len(gots),
        "hots": len(hots),
        "rounds": rounds,
        "jobs": jobs,
        "before": list(before),
        "after": after,
        "full": list(full),
        "lags": lags is not None,
        "summed": summed,
        "widens": keep.dtype != F32,
    }
    out = [jax.ShapeDtypeStruct((2, NB, LANES), F32)] * len(after)
    scratch = [pltpu.VMEM((len(gots), 2, width // summed // 2, pairs, 2 * LANES), BF16)]
    inputs = [keep, *gots, *hots, *before.values()]
    specs = [VMEM] * len(inputs)
    if full:
        inputs, specs = inputs + [table], specs + [HBM]
        out.append(jax.ShapeDtypeStruct((NB, LAGS), lags_type))
        scratch += [
            pltpu.VMEM((2, len(full) * 2 * LANES, LAGS), BF16),
            pltpu.VMEM((len(full), 2, NB, LANES), F32),
            pltpu.SemaphoreType.DMA((2,)),
        ]
    if lags is not None:
        inputs, specs = inputs + [lags], specs + [VMEM]
    if keep.dtype != F32:
        out.append(jax.ShapeDtypeStruct(keep.shape, F32))
    if gives_hots:
        out += [jax.ShapeDtypeStruct((2, NB, pairs), BF16)] * len(rounds)
    else:
        scratch = [pltpu.VMEM((2, NB, pairs), BF16)] * len(rounds) + scratch
    results = pl.pallas_call(
        functools.partial(stage_kernel, plan),
        out_shape=out,
        in_specs=specs,
        out_specs=[VMEM] * len(out),
        scratch_shapes=scratch,
        compiler_params=PARAMS,
        name="stage",
    )(*inputs)
    count = len(after)
    lags_out = results[count] if full else None
    return dict(zip(after, results)), list(results[count + bool(full) :]), lags_out


def sum_kernel(scaling, parts_ref, out_ref):
    total = parts_ref[0].astype(F32)
    for source in range(1, parts_ref.shape[0]):
        total = total + parts_ref[source].astype(F32)
    out_ref[...] = total * scaling


def summed(parts, scaling):
    return pl.pallas_call(
        functools.partial(sum_kernel, scaling),
        out_shape=jax.ShapeDtypeStruct(parts.shape[1:], F32),
        in_specs=[VMEM],
        out_specs=VMEM,
        compiler_params=PARAMS,
        name="summed",
    )(parts)


def build_table(freq_len):
    freq_ids = np.arange(freq_len).reshape(2, freq_len // 2 // LANES, 1, LANES)
    lag_ids = np.arange(LAGS) - LAGS // 2
    angles = (freq_ids[..., None] * lag_ids % NT) * (2.0 * math.pi / NT)
    weights = np.where(freq_ids == 0, 1.0, 2.0)[..., None]
    table = np.concatenate([weights * np.cos(angles), -weights * np.sin(angles)], axis=2)
    table = table.reshape(2, freq_len, LAGS).astype(np.float32)
    high = table.astype(BF16)
    return np.stack([high, (table - high.astype(np.float32)).astype(BF16)], axis=1)


def on_device(spectra, pair_bins, dead_mask):
    block, width, columns = spectra.shape
    freq_len = columns // 2
    groups = lax.axis_size("row") * lax.axis_size("col")
    table = jnp.asarray(build_table(freq_len))
    tile_planes = 2 * width

    def send(value, round_no):
        return swapped(value, round_no, groups)

    first, second, whole, keep = whiten(spectra, pair_bins, dead_mask, 2)
    core, far_first = send(whole, 0), send(first, 2)
    core, to_near = lax.optimization_barrier((core, first))
    near_first = send(to_near, 1)
    across_first, across_second = send(first, 3), send(second, 3)

    def planes(tiles, gots=1):
        return [(tile, ((tile - tiles[0]) * tile_planes,) * gots) for tile in tiles]

    sums, (keep,), _ = stage(width, keep, [core], [], [0], planes((0, 1, 2)), {})
    work = functools.partial(stage, width, keep)
    low, across_hots, _ = work([across_first], [], [3], planes((0, 1)), {0: sums[0], 1: sums[1]}, gives_hots=True)
    high, _, _ = work([across_second], across_hots, [], planes((2,)), {2: sums[2]})
    second, low, high = lax.optimization_barrier((second, low, high))
    far_second, near_second = send(second, 2), send(second, 1)
    _, hots, lags = work([far_first, near_first], [], [2, 1], planes((0, 1), 2), low, (0, 1), table, gives_hots=True)
    _, _, lags = work([far_second, near_second], hots, [], planes((2,), 2), high, (2,), table, lags, BF16, summed=2 * SUMMED)
    mine = lax.all_to_all(lags.reshape(groups, NB // groups, LAGS), AXES, 0, 0, tiled=True)
    pairs = ROUNDS * block * block * groups // NB
    return summed(mine, 1.0 / (2.0 * math.sqrt(freq_len * width * pairs)))


def solution(mesh):
    return jax.shard_map(
        on_device,
        mesh=mesh,
        in_specs=(P(AXES, None, None), P(None, AXES, None), P(AXES)),
        out_specs=P(AXES, None),
        check_vma=False,
    )
```

```python
import functools
import math

import jax
import jax.numpy as jnp
import numpy as np
from jax import lax
from jax.experimental import pallas as pl
from jax.experimental.pallas import tpu as pltpu
from jax.sharding import PartitionSpec as P

NT = 1600
LAGS = 896
NB = 128
ROUNDS = 4
LANES = 128
ROWS = 16
STEP = 16
SUMMED = 2
AXES = ("row", "col")
F32 = jnp.float32
BF16 = jnp.bfloat16
VMEM = pl.BlockSpec(memory_space=pltpu.VMEM)
HBM = pl.BlockSpec(memory_space=pltpu.MemorySpace.HBM)
LARGE = pltpu.CompilerParams(vmem_limit_bytes=63488 * 2**10)
PARAMS = pltpu.CompilerParams(vmem_limit_bytes=48 * 2**20)


def parity_of(index):
    total = 0
    for bit in range(ROUNDS):
        total = total + ((index >> bit) & 1)
    return total % 2


def half_here():
    return parity_of(lax.axis_index("row") * lax.axis_size("col") + lax.axis_index("col"))


def swapped(value, stride, groups):
    mask = 2**stride
    return lax.ppermute(value, AXES, [(source, source ^ mask) for source in range(groups)])


def one_hot(rows, columns, row_offset, of_column):
    row_ids = lax.broadcasted_iota(jnp.int32, (rows, columns), 0)
    column_ids = lax.broadcasted_iota(jnp.int32, (rows, columns), 1)
    return (row_ids == row_offset + of_column(column_ids)).astype(BF16)


def plane_of(scaled_ref, plane, block, half):
    tiles, width = scaled_ref.shape[0] // 4, scaled_ref.shape[1] // block
    tile, window, part = plane // (2 * width), plane // 2 % width, plane % 2
    return scaled_ref[2 * tiles * part + tiles * half + tile, pl.ds(window, block, stride=width), :]


def whiten_kernel(spectra_ref, bins_ref, alive_ref, *refs):
    (first_ref, second_ref, whole_ref, keep_ref), refs = refs[:4], refs[4:]
    scaled_ref, loaded_ref, loaded_bins_ref, loaded_alive_ref, sent_ref, kept_ref, sems, out_sems = refs
    block, width, columns = spectra_ref.shape
    copies = [
        pltpu.make_async_copy(spectra_ref.at[pl.ds(at, STEP)], loaded_ref.at[pl.ds(at, STEP)], sems.at[at // STEP])
        for at in range(0, block, STEP)
    ]
    bins_copy = pltpu.make_async_copy(bins_ref, loaded_bins_ref, sems.at[block // STEP])
    alive_copy = pltpu.make_async_copy(alive_ref, loaded_alive_ref, sems.at[block // STEP + 1])
    for copy in [bins_copy, alive_copy, *copies]:
        copy.start()
    half = half_here()
    planes = sent_ref.shape[0] - 1
    firsts = first_ref.shape[0] - 1
    bins_copy.wait()
    bins = jnp.zeros((block, LANES), F32)
    for round_no in range(bins_ref.shape[0]):
        place = one_hot(block, LANES, -block * round_no, lambda ids: ids)
        bins = bins + jnp.dot(loaded_bins_ref[round_no].astype(F32).astype(BF16), place, preferred_element_type=F32)
    sent_ref[planes] = bins.astype(BF16)
    kept_ref[planes] = bins.astype(BF16)
    for channel in range(block):
        if channel % STEP == 0:
            copies[channel // STEP].wait()
        if channel == 0:
            alive_copy.wait()
        values = loaded_ref[channel].astype(F32)
        powers = jnp.mean(values * values, axis=-1, keepdims=True)
        values = values * (lax.rsqrt(powers + 1e-06) * loaded_alive_ref[channel].astype(F32))
        for tile in range(columns // LANES):
            scaled_ref[tile, channel * width : (channel + 1) * width, :] = values[:, tile * LANES : (tile + 1) * LANES]
    going = []

    def go(source, target):
        going.append(pltpu.make_async_copy(source, target, out_sems.at[len(going)]))
        going[-1].start()

    for plane in range(planes):
        sent_ref[plane] = plane_of(scaled_ref, plane, block, 1 - half).astype(BF16)
        if plane == firsts - 1:
            go(sent_ref.at[pl.ds(0, firsts)], first_ref.at[pl.ds(0, firsts)])
            go(sent_ref.at[pl.ds(planes, 1)], first_ref.at[pl.ds(firsts, 1)])
    go(sent_ref, whole_ref)
    go(sent_ref.at[pl.ds(firsts, planes - firsts)], second_ref)
    for plane in range(planes):
        kept_ref[plane] = plane_of(scaled_ref, plane, block, half).astype(BF16)
    go(kept_ref, keep_ref)
    for copy in going:
        copy.wait()


def whiten(spectra, bins, alive, first_tiles):
    block, width, columns = spectra.shape
    planes = columns // 2 // LANES * width
    firsts = first_tiles * 2 * width

    def sent(count):
        return jax.ShapeDtypeStruct((count, block, LANES), BF16)

    return pl.pallas_call(
        whiten_kernel,
        out_shape=(sent(firsts + 1), sent(planes - firsts), sent(planes + 1), sent(planes + 1)),
        in_specs=[HBM, HBM, HBM],
        out_specs=(HBM,) * 4,
        scratch_shapes=[
            pltpu.VMEM((columns // LANES, block * width, LANES), F32),
            pltpu.VMEM(spectra.shape, BF16),
            pltpu.VMEM(bins.shape, jnp.int32),
            pltpu.SMEM(alive.shape, jnp.int32),
            pltpu.VMEM((planes + 1, block, LANES), BF16),
            pltpu.VMEM((planes + 1, block, LANES), BF16),
            pltpu.SemaphoreType.DMA((block // STEP + 2,)),
            pltpu.SemaphoreType.DMA((5,)),
        ],
        compiler_params=LARGE,
        name="whiten",
    )(spectra, bins, alive)


def hot_pairs(mine, theirs, round_no, block):
    pairs = block * block
    base = block * round_no
    rows = lax.broadcasted_iota(jnp.int32, (block, pairs), 0)
    columns = lax.broadcasted_iota(jnp.int32, (block, pairs), 1)
    by_second = jnp.dot(mine, one_hot(LANES, pairs, base, lambda ids: ids % block), preferred_element_type=F32)
    by_first = jnp.dot(theirs, one_hot(LANES, pairs, base, lambda ids: ids // block), preferred_element_type=F32)
    first = jnp.sum(jnp.where(rows == columns // block, by_second, 0.0), axis=0, keepdims=True)
    second = jnp.sum(jnp.where(rows == columns % block, by_first, 0.0), axis=0, keepdims=True)
    bin_ids = lax.broadcasted_iota(jnp.int32, (NB, pairs), 0).astype(F32).astype(BF16)
    one, zero = jnp.ones((NB, pairs), BF16), jnp.zeros((NB, pairs), BF16)
    hot_first = jnp.where(bin_ids == jnp.broadcast_to(first.astype(BF16), (NB, pairs)), one, zero)
    hot_second = jnp.where(bin_ids == jnp.broadcast_to(second.astype(BF16), (NB, pairs)), one, zero)
    return hot_first + hot_second, hot_first - hot_second


def products(keep_ref, gots, cross_ref, width, summed, here):
    block = keep_ref.shape[1]

    def of_channel(channel, carry):
        for some in range(width // summed):
            sums = {}
            for window in range(some * summed, (some + 1) * summed):
                one_real, one_imag = [
                    jnp.broadcast_to(keep_ref[here + 2 * window + k, pl.ds(channel, 1), :], (ROWS, LANES)).astype(BF16)
                    for k in range(2)
                ]
                for number, (got_ref, there) in enumerate(gots):
                    for start in range(0, block, ROWS):
                        two_real = got_ref[there + 2 * window, start : start + ROWS, :]
                        two_imag = got_ref[there + 2 * window + 1, start : start + ROWS, :]
                        real = one_real * two_real + one_imag * two_imag
                        imag = one_imag * two_real - one_real * two_imag
                        old = sums.get((number, start))
                        sums[number, start] = (real, imag) if old is None else (old[0] + real, old[1] + imag)
            lanes = slice(some % 2 * LANES, (some % 2 + 1) * LANES)
            for (number, start), pair in sums.items():
                at = pl.ds(pl.multiple_of(channel * block + start, ROWS), ROWS)
                for part in range(2):
                    cross_ref[number, part, some // 2, at, lanes] = pair[part]
        return carry

    lax.fori_loop(0, block, of_channel, 0, unroll=8 // len(gots))


def binned(hots_refs, cross_ref, part):
    total = None
    for number, hots_ref in enumerate(hots_refs):
        for some in range(cross_ref.shape[2]):
            more = jnp.dot(hots_ref[part], cross_ref[number, part, some], preferred_element_type=F32)
            total = more if total is None else total + more
    return total[:, :LANES] + total[:, LANES:]


def table_copies(table_ref, loaded_ref, sems, start):
    rows = loaded_ref.shape[1]
    half = half_here()
    return [
        pltpu.make_async_copy(table_ref.at[half, level, pl.ds(start, rows)], loaded_ref.at[level], sems.at[level])
        for level in range(2)
    ]


def lags_of(sums, loaded_ref):
    values = jnp.concatenate(sums, axis=1)
    high = values.astype(BF16)
    low = (values - high.astype(F32)).astype(BF16)
    both = jnp.dot(jnp.concatenate([high, low], axis=0), loaded_ref[0], preferred_element_type=F32)
    return both[:NB] + both[NB:] + jnp.dot(high, loaded_ref[1], preferred_element_type=F32)


def stage_kernel(plan, *refs):
    refs = iter(refs)
    take = lambda count: [next(refs) for _ in range(count)]
    (keep_ref,), got_refs = take(1), take(plan["gots"])
    hots_refs, before_refs = take(plan["hots"]), take(len(plan["before"]))
    table_ref = next(refs) if plan["full"] else None
    lags_ref = next(refs) if plan["lags"] else None
    after_refs = take(len(plan["after"]))
    out_ref = next(refs) if plan["full"] else None
    wide_ref = next(refs) if plan["widens"] else None
    hots_refs = hots_refs + take(len(plan["rounds"]))
    if plan["widens"]:
        wide_ref[...] = keep_ref[...].astype(F32)
        keep_ref = wide_ref
    cross_ref = next(refs)
    width = plan["width"]
    if plan["full"]:
        loaded_ref, sums_ref, sems = take(3)
        copies = table_copies(table_ref, loaded_ref, sems, min(plan["full"]) * 2 * LANES)
        for copy in copies:
            copy.start()
    for round_no, got_ref, hots_ref in zip(plan["rounds"], got_refs, hots_refs):
        mine, theirs = keep_ref[keep_ref.shape[0] - 1].astype(BF16), got_ref[got_ref.shape[0] - 1]
        plus, minus = hot_pairs(mine, theirs, round_no, keep_ref.shape[1])
        hots_ref[0] = plus
        hots_ref[1] = minus
    places = {tile: ref for tile, ref in zip(plan["before"], before_refs)}
    for tile, starts in plan["jobs"]:
        products(keep_ref, list(zip(got_refs, starts)), cross_ref, width, plan["summed"], tile * 2 * width)
        to = after_refs[plan["after"].index(tile)] if tile in plan["after"] else sums_ref.at[plan["full"].index(tile)]
        for part in range(2):
            sums = binned(hots_refs, cross_ref, part)
            to[part] = sums + places[tile][part] if tile in places else sums
        places[tile] = to
    if plan["full"]:
        sums = [places[tile][part] for tile in plan["full"] for part in range(2)]
        for copy in copies:
            copy.wait()
        lags = lags_of(sums, loaded_ref)
        if lags_ref is not None:
            lags = lags + lags_ref[...]
        out_ref[...] = lags.astype(out_ref.dtype)


def stage(width, keep, gots, hots, rounds, jobs, before, full=(), table=None, lags=None, lags_type=F32, gives_hots=False, summed=SUMMED):
    block = keep.shape[1]
    pairs = block * block
    after = [tile for tile, _ in jobs if tile not in full]
    plan = {
        "width": width,
        "gots": len(gots),
        "hots": len(hots),
        "rounds": rounds,
        "jobs": jobs,
        "before": list(before),
        "after": after,
        "full": list(full),
        "lags": lags is not None,
        "summed": summed,
        "widens": keep.dtype != F32,
    }
    out = [jax.ShapeDtypeStruct((2, NB, LANES), F32)] * len(after)
    scratch = [pltpu.VMEM((len(gots), 2, width // summed // 2, pairs, 2 * LANES), BF16)]
    inputs = [keep, *gots, *hots, *before.values()]
    specs = [VMEM] * len(inputs)
    if full:
        inputs, specs = inputs + [table], specs + [HBM]
        out.append(jax.ShapeDtypeStruct((NB, LAGS), lags_type))
        scratch += [
            pltpu.VMEM((2, len(full) * 2 * LANES, LAGS), BF16),
            pltpu.VMEM((len(full), 2, NB, LANES), F32),
            pltpu.SemaphoreType.DMA((2,)),
        ]
    if lags is not None:
        inputs, specs = inputs + [lags], specs + [VMEM]
    if keep.dtype != F32:
        out.append(jax.ShapeDtypeStruct(keep.shape, F32))
    if gives_hots:
        out += [jax.ShapeDtypeStruct((2, NB, pairs), BF16)] * len(rounds)
    else:
        scratch = [pltpu.VMEM((2, NB, pairs), BF16)] * len(rounds) + scratch
    results = pl.pallas_call(
        functools.partial(stage_kernel, plan),
        out_shape=out,
        in_specs=specs,
        out_specs=[VMEM] * len(out),
        scratch_shapes=scratch,
        compiler_params=PARAMS,
        name="stage",
    )(*inputs)
    count = len(after)
    lags_out = results[count] if full else None
    return dict(zip(after, results)), list(results[count + bool(full) :]), lags_out


def sum_kernel(scaling, parts_ref, out_ref):
    total = parts_ref[0].astype(F32)
    for source in range(1, parts_ref.shape[0]):
        total = total + parts_ref[source].astype(F32)
    out_ref[...] = total * scaling


def summed(parts, scaling):
    return pl.pallas_call(
        functools.partial(sum_kernel, scaling),
        out_shape=jax.ShapeDtypeStruct(parts.shape[1:], F32),
        in_specs=[VMEM],
        out_specs=VMEM,
        compiler_params=PARAMS,
        name="summed",
    )(parts)


def build_table(freq_len):
    freq_ids = np.arange(freq_len).reshape(2, freq_len // 2 // LANES, 1, LANES)
    lag_ids = np.arange(LAGS) - LAGS // 2
    angles = (freq_ids[..., None] * lag_ids % NT) * (2.0 * math.pi / NT)
    weights = np.where(freq_ids == 0, 1.0, 2.0)[..., None]
    table = np.concatenate([weights * np.cos(angles), -weights * np.sin(angles)], axis=2)
    table = table.reshape(2, freq_len, LAGS).astype(np.float32)
    high = table.astype(BF16)
    return np.stack([high, (table - high.astype(np.float32)).astype(BF16)], axis=1)


def on_device(spectra, pair_bins, dead_mask):
    block, width, columns = spectra.shape
    freq_len = columns // 2
    groups = lax.axis_size("row") * lax.axis_size("col")
    table = jnp.asarray(build_table(freq_len))
    tile_planes = 2 * width

    def send(value, round_no):
        return swapped(value, round_no, groups)

    first, second, whole, keep = whiten(spectra, pair_bins, dead_mask, 2)
    core, far_first = send(whole, 0), send(first, 2)
    core, to_near = lax.optimization_barrier((core, first))
    near_first = send(to_near, 1)
    across_first, across_second = send(first, 3), send(second, 3)

    def planes(tiles, gots=1):
        return [(tile, ((tile - tiles[0]) * tile_planes,) * gots) for tile in tiles]

    sums, (keep,), _ = stage(width, keep, [core], [], [0], planes((0, 1, 2)), {})
    work = functools.partial(stage, width, keep)
    low, across_hots, _ = work([across_first], [], [3], planes((0, 1)), {0: sums[0], 1: sums[1]}, gives_hots=True)
    high, _, _ = work([across_second], across_hots, [], planes((2,)), {2: sums[2]})
    second, low, high = lax.optimization_barrier((second, low, high))
    far_second, near_second = send(second, 2), send(second, 1)
    _, hots, lags = work([far_first, near_first], [], [2, 1], planes((0, 1), 2), low, (0, 1), table, gives_hots=True)
    _, _, lags = work([far_second, near_second], hots, [], planes((2,), 2), high, (2,), table, lags, BF16, summed=2 * SUMMED)
    mine = lax.all_to_all(lags.reshape(groups, NB // groups, LAGS), AXES, 0, 0, tiled=True)
    pairs = ROUNDS * block * block * groups // NB
    return summed(mine, 1.0 / (2.0 * math.sqrt(freq_len * width * pairs)))


def solution(mesh):
    return jax.shard_map(
        on_device,
        mesh=mesh,
        in_specs=(P(AXES, None, None), P(None, AXES, None), P(AXES)),
        out_specs=P(AXES, None),
        check_vma=False,
    )
```
